256 devices in a mesh: ka: 32 (over z, y), tau: 8 (over x, core).
Axes of the slice: x: 4, y: 4, z: 8, core: 2. Of those that a mesh axis runs over, the one named last changes fastest.
Arguments:
- green: bfloat16 [64, 8, 128, 128], P('ka', 'tau'), may hold values from -6 to 6
- chol: bfloat16 [128, 600, 128, 128], P('ka', 'tau'), may hold values from -0.375 to 0.375
- triplets: int32 [64, 4], replicated, may hold values from 0 to 63, as said below
- diff: int32 [64, 64], replicated, may hold values from 0 to 63, as said below
Outputs:
- sigma: float32 [64, 8, 128, 128], P('ka', 'tau')
The draws below stay inside these ranges and needn't reach their ends.
Inputs may be any that keep to these rules, and one draw needn't show every extreme that they name: Columns are k1, k2, k3 and owner, a ka index. An owner holds 0 to 4 triplets and some owner holds exactly 4; chol slot owner * 4 + r belongs to that owner's r-th triplet in list order. No two triplets of one owner have k1 // 2 equal. diff[a, b] is the k-point whose lattice vector is that of a minus that of b modulo a mesh of 4 x 4 x 64//16 points; k-points carry permuted labels.
All inputs are finite; a program needn't handle non-finite values.
Results may differ from the reference program's by a relative error of at most 0.0006.
Values may be sent and summed in bfloat16 or wider, within the bound.
A program may use at most 64 MiB of HBM per device.

```python
import jax
import jax.numpy as jnp
from jax import lax

NORB = 128
NAUX = 600
KDEV = 2
TRIP_DEV = 2
CAP = 4
NK = 64
NTAU = 8
NTRIP = 64
SLOTS = 128
N_KA = 32


def draw_triplets(key, part):
    key = jax.random.fold_in(key, 11)
    keys = jax.random.split(key, 6)
    pattern = jnp.array([2, 1, 1, 0], jnp.int32) * TRIP_DEV
    counts = jnp.tile(pattern, N_KA // 4)
    owner_of_rank = jax.random.permutation(keys[0], N_KA).astype(jnp.int32)
    rank_of_row = jnp.repeat(jnp.arange(N_KA, dtype=jnp.int32), counts, total_repeat_length=NTRIP)
    owners = owner_of_rank[rank_of_row]
    starts = jnp.cumsum(counts) - counts
    within = jnp.arange(NTRIP, dtype=jnp.int32) - starts[rank_of_row]
    scores = jax.random.randint(keys[1], (N_KA, N_KA), 0, 1 << 20) * N_KA + jnp.arange(N_KA, dtype=jnp.int32)[None, :]
    device_order = jnp.argsort(scores, axis=1).astype(jnp.int32)
    first_device = device_order[owners, within]
    first = first_device * KDEV + jax.random.randint(keys[2], (NTRIP,), 0, KDEV)
    second = jax.random.randint(keys[3], (NTRIP,), 0, NK)
    third = jax.random.randint(keys[4], (NTRIP,), 0, NK)
    second = second.at[0].set(NK - 1)
    third = third.at[0].set(0)
    table = jnp.stack([first, second, third, owners], axis=1).astype(jnp.int32)
    shuffle = jax.random.permutation(keys[5], NTRIP)
    return table[shuffle]


def draw_diff(key, part):
    key = jax.random.fold_in(key, 23)
    depth = NK // 16
    labels = jax.random.permutation(key, NK).astype(jnp.int32)
    inverse = jnp.argsort(labels).astype(jnp.int32)
    coord_x = labels // (4 * depth)
    coord_y = labels // depth % 4
    coord_z = labels % depth
    delta_x = (coord_x[:, None] - coord_x[None, :]) % 4
    delta_y = (coord_y[:, None] - coord_y[None, :]) % 4
    delta_z = (coord_z[:, None] - coord_z[None, :]) % depth
    point = delta_x * (4 * depth) + delta_y * depth + delta_z
    return inverse[point].astype(jnp.int32)


def block_levels(own_key, shape, pieces, smallest, largest):
    level, own = 1.0, jax.random.fold_in(own_key, 6)
    for dim, blocks in pieces:
        draws = jnp.exp(jax.random.uniform(jax.random.fold_in(own, dim), (blocks,), jnp.float32, smallest / len(pieces), largest / len(pieces)))
        level = level * jnp.repeat(draws, shape[dim] // blocks).reshape([-1 if axis == dim else 1 for axis in range(len(shape))])
    return level


def bell_draw(stream_key, shape, deviation, limit, shards=(), kind=jnp.bfloat16):
    entries = jax.random.normal(stream_key, shape, jnp.float32) * deviation
    if len(shards) > 0:
        entries = block_levels(stream_key, shape, shards, -0.22, 0.18) * entries
    return jnp.clip(entries, min=-limit, max=limit).astype(kind)


def setup_inputs(seed: int = 0) -> dict:
    arg_keys = jax.random.split(jax.random.key(seed), 5)
    return {
        "green": bell_draw(arg_keys[0], (NK, NTAU, NORB, NORB), 1.0, 6.0, ((0, 32), (1, 8))),
        "chol": bell_draw(arg_keys[1], (SLOTS, NAUX, NORB, NORB), (2 * NORB) ** -0.5, 0.375, ((0, 32), (1, 8))),
        "triplets": draw_triplets(jax.random.fold_in(arg_keys[4], 71), 0),
        "diff": draw_diff(jax.random.fold_in(arg_keys[4], 71), 0),
    }


def aux_block(total):
    best = 1
    for cand in range(1, min(total, 64) + 1):
        if total % cand == 0:
            best = cand
    return best


def reference(green, chol, triplets, diff):
    first = triplets[:, 0]
    second = triplets[:, 1]
    third = triplets[:, 2]
    owners = triplets[:, 3]
    order = jnp.arange(NTRIP, dtype=jnp.int32)
    same = (owners[:, None] == owners[None, :]) & (order[:, None] > order[None, :])
    ranks = jnp.sum(same.astype(jnp.int32), axis=1)
    slots = (owners * CAP + ranks).astype(jnp.int32)
    fourth = diff[first, diff[second, third]].astype(jnp.int32)
    rows = jnp.stack([first, second, fourth, slots], axis=1).astype(jnp.int32)
    block = aux_block(NAUX)

    def step(sigma, row):
        vectors = lax.dynamic_index_in_dim(chol, row[3], 0, keepdims=False)
        near = lax.dynamic_index_in_dim(green, row[1], 0, keepdims=False).astype(jnp.float32)
        far = lax.dynamic_index_in_dim(green, row[2], 0, keepdims=False).astype(jnp.float32)
        groups = vectors.reshape(NAUX // block, block, NORB, NORB).astype(jnp.float32)

        def inner(total, piece):
            product = jnp.einsum('qij,tjl->tqil', piece, near)
            return total + jnp.einsum('tqil,qil->til', product, piece), None

        summed, unused = lax.scan(inner, jnp.zeros((NTAU, NORB, NORB), jnp.float32), groups)
        current = lax.dynamic_index_in_dim(sigma, row[0], 0, keepdims=False)
        sigma = lax.dynamic_update_index_in_dim(sigma, current + summed * far, row[0], 0)
        return sigma, None

    sigma, unused = lax.scan(step, jnp.zeros((NK, NTAU, NORB, NORB), jnp.float32), rows)
    return sigma
```

```python
import jax
import jax.numpy as jnp
from jax import lax
from jax.experimental import pallas as pl
from jax.experimental.pallas import tpu as pltpu
from jax.sharding import PartitionSpec as P

MESH = pl.DeviceIdType.MESH
ZN, YN, XN, CAP = 8, 4, 4, 4
F32 = jnp.float32
FIRST = (0,)
LAST = (1, 2, 3)
CHUNKS = ((0, 48), (48, 32), (80, 32), (112, 16))
LEVELS = 32766.0
PAIRS = (((0, 0), (1, 0)), ((0, 1), (0, 3)), ((0, 2), (1, 2)), ((1, 1), (1, 3)))


def contract_pair(vectors, near, results, pair, at, step, row):
    x = vectors[:, pl.ds(at, step), :]
    count, _, width = x.shape
    weight = jnp.concatenate([near[e, d] for e, d in pair], axis=1)
    product = jnp.dot(
        x.reshape(count * step, width), weight, preferred_element_type=F32
    ).reshape(count, step, 2 * width)
    wide = x.astype(F32)
    total = jnp.zeros((step, 2 * width), F32)
    for q in range(count):
        total = total + product[q] * jnp.concatenate([wide[q], wide[q]], axis=1)
    for i, (e, d) in enumerate(pair):
        results[e][d, pl.ds(row, step), :] = total[:, i * width : (i + 1) * width]


def kernel(trip_hbm, diff_hbm, green, chol, out, *scratch):
    g = dict(zip(list(SCRATCH), scratch))
    ka = lax.axis_index("ka")
    tau = lax.axis_index("tau")
    z, y = ka // YN, ka % YN
    x, core = tau // 2, tau % 2
    units = [("f%d" % s, (s,), 0, 128) for s in FIRST]
    units += [("c%d" % c, LAST, r0, rows) for c, (r0, rows) in enumerate(CHUNKS)]

    def zdev(d):
        return {"ka": (z + d) % ZN * YN + y}

    def ydev(d):
        return {"ka": z * YN + (y + d) % YN}

    def xdev(d):
        return {"tau": (x + d) % XN * 2 + core}

    sibling = {"tau": x * 2 + 1 - core}

    barrier = pltpu.get_barrier_semaphore()
    peers = [zdev(d) for d in range(1, ZN)] + [ydev(d) for d in range(1, YN)]
    peers += [xdev(d) for d in range(1, XN)] + [sibling]
    for peer in peers:
        pl.semaphore_signal(barrier, inc=1, device_id=peer, device_id_type=MESH)

    ring = [g["ring%d" % d] for d in range(ZN)]
    trip, diff = g["trip"], g["diff"]
    first_loads = [
        pltpu.make_async_copy(green.at[:, 0], ring[0], g["first_sem"].at[0]),
        pltpu.make_async_copy(trip_hbm, trip, g["first_sem"].at[1]),
        pltpu.make_async_copy(diff_hbm, diff, g["first_sem"].at[2]),
    ]
    loads = [
        pltpu.make_async_copy(chol.at[s], g["chol%d" % s], g["chol_sem"].at[s]) for s in range(CAP)
    ]
    for load in first_loads + loads:
        load.start()
    for load in first_loads:
        load.wait()
    pl.semaphore_wait(barrier, len(peers))

    sends = []

    def copy_to(src, dst, name, index, where):
        return pltpu.make_async_remote_copy(
            src_ref=src, dst_ref=dst, send_sem=g[name + "_s"].at[index], recv_sem=g[name + "_r"].at[index],
            device_id=where, device_id_type=MESH,
        )

    def go(*args):
        copy = copy_to(*args)
        copy.start()
        sends.append(copy)

    def hop(way, step, kk):
        if way == 0:
            src, dst, to = ring[step - 1], ring[step], zdev(1)
        else:
            src, dst, to = ring[(ZN + 1 - step) % ZN], ring[ZN - step], zdev(ZN - 1)
        return src.at[kk], dst.at[kk], "ring", (way * ZN + step) * 2 + kk, to

    def hops(step):
        if step < ZN // 2:
            return [(way, step, kk) for kk in range(2) for way in range(2)]
        return [(0, step, 0), (1, step, 1)]

    for args in hops(1):
        go(*hop(*args))

    def scan(t, carry):
        counts, found = carry
        owner = trip[3, t]
        row_hit = (owner // YN) == z
        rel = (owner % YN + YN - y) % YN
        new_counts, new_found = [], []
        for j in range(YN):
            hit = row_hit & (rel == j)
            for s in range(CAP):
                new_found.append(jnp.where(hit & (counts[j] == s), t, found[j * CAP + s]))
            new_counts.append(counts[j] + hit.astype(jnp.int32))
        return tuple(new_counts), tuple(new_found)

    zero = jnp.int32(0)
    state = ((zero,) * YN, (zero,) * (YN * CAP))
    rows_of = trip.shape[1]
    half = ZN // 2
    for step in range(1, half + 1):
        state = lax.fori_loop((step - 1) * rows_of // half, step * rows_of // half, scan, state)
        if step < half:
            ahead = hops(step + 1)
            for way, _, kk in hops(step):
                copy_to(*hop(way, step, kk)).wait_recv()
                if (way, step + 1, kk) in ahead:
                    go(*hop(way, step + 1, kk))
    counts, found = state
    tab = g["tab"]
    firsts = []
    for j in range(YN):
        for s in range(CAP):
            row = found[j * CAP + s]
            k1, k2, k3 = trip[0, row], trip[1, row], trip[2, row]
            for which, k in enumerate((k2, diff[k1, diff[k2, k3]])):
                tab[((j * CAP + s) * 2 + which) * 2] = (z + ZN - k // (2 * YN)) % ZN * 2 + k % 2
                tab[((j * CAP + s) * 2 + which) * 2 + 1] = (y + YN - k // 2 % YN) % YN
            firsts.append(jnp.where(counts[j] > s, k1, -1))
    for way, step, kk in hops(half):
        copy_to(*hop(way, step, kk)).wait_recv()
    pool = g["pool"]
    for d in range(ZN):
        for kk in range(2):
            pool[2 * d + kk] = ring[d][kk]

    def pick(j, s, which):
        return pool[tab[((j * CAP + s) * 2 + which) * 2]]

    def spread(s, which):
        tag = "nf"[which]
        send, recv = g["%ssend%d" % (tag, s)], g["%srecv%d" % (tag, s)]
        for d in range(1, YN):
            send[d - 1] = pick(d, s, which)
            go(send.at[d - 1], recv.at[d], tag, s * YN + d, ydev(d))
        recv[0] = pick(0, s, which)

    def collect(s, which):
        tag = "nf"[which]
        send, recv = g["%ssend%d" % (tag, s)], g["%srecv%d" % (tag, s)]
        for d in range(1, YN):
            copy_to(send.at[d - 1], recv.at[d], tag, s * YN + d, ydev(d)).wait_recv()
        rel = tab[(s * 2 + which) * 2 + 1]
        block = recv[0]
        for d in range(1, YN):
            block = jnp.where(rel == d, recv[d], block)
        return block

    near = [g["near%d" % s] for s in range(CAP)]

    def near_out(s):
        near[s][0, 0] = collect(s, 0)
        go(near[s].at[0, 0], near[s].at[1, 0], "w", s * XN, sibling)
        for d in (1, XN - 1, 2):
            go(near[s].at[0, 0], near[s].at[0, d], "x", s * XN + d, xdev(d))

    def near_on(s):
        for d in (1, XN - 1, 2):
            copy_to(near[s].at[0, 0], near[s].at[0, d], "x", s * XN + d, xdev(d)).wait_recv()
            go(near[s].at[0, d], near[s].at[1, d], "w", s * XN + d, sibling)

    def near_in(s, *ds):
        for d in ds:
            copy_to(near[s].at[0, d], near[s].at[1, d], "w", s * XN + d, sibling).wait_recv()

    def compute(name, s, j, r0, rows, pairs=PAIRS):
        results = [g[k + name].at[:, j] for k in ("keep_", "give_")]
        for pair in pairs:
            for row in range(0, rows, 16):
                contract_pair(g["chol%d" % s], near[s], results, pair, r0 + row, 16, row)

    def sib_out(name):
        go(g["give_" + name], g["sib_" + name], "sib_" + name, 0, sibling)

    def x_out(name):
        keep, sib, sums, recv = (g[k + name] for k in ("keep_", "sib_", "sums_", "xr_"))
        copy_to(g["give_" + name], sib, "sib_" + name, 0, sibling).wait_recv()
        for d in range(1, XN):
            sums[d] = keep[d] + sib[d]
            go(sums.at[d], recv.at[d], "xr_" + name, d, xdev(XN - d))

    def y_out(name, slots, r0, rows):
        keep, sib, sums, recv, own, cand = (
            g[k + name] for k in ("keep_", "sib_", "sums_", "xr_", "own_", "cand_")
        )
        for d in range(1, XN):
            copy_to(sums.at[d], recv.at[d], "xr_" + name, d, xdev(XN - d)).wait_recv()
        for j, s in enumerate(slots):
            total = keep[0, j] + sib[0, j]
            for d in range(1, XN):
                total = total + recv[d, j]
            own[j] = total * g["far%d" % s][pl.ds(r0, rows), :].astype(F32)
        for d in range(1, YN):
            go(own, cand.at[d], "cand_" + name, d, ydev(d))

    def y_in(name):
        for d in range(1, YN):
            copy_to(g["own_" + name], g["cand_" + name].at[d], "cand_" + name, d, ydev(d)).wait_recv()

    route = g["route"]

    def make_routes():
        for dz in range(ZN):
            target = (z + dz) % ZN * YN + y
            for d in range(YN):
                j = (YN - d) % YN
                code = jnp.int32(8)
                for s in range(CAP):
                    k1 = firsts[j * CAP + s]
                    code = jnp.where((k1 >= 0) & ((k1 // 2) == target), s * 2 + k1 % 2, code)
                route[dz * YN + d] = code

    def sums_for(dz, local):
        sums = [jnp.zeros(local.shape[2:], F32) for _ in range(2)]
        for d in range(YN):
            code = route[dz * YN + d]
            block = local[d, (code % 8) // 2]
            for kk in range(2):
                sums[kk] = sums[kk] + jnp.where((code < 8) & (code % 2 == kk), block, 0.0)
        return sums

    def z_out(c):
        name, slots, r0, rows = units[len(FIRST) + c]
        y_in(name)
        local = g["local_" + name]
        for d in range(YN):
            for s in FIRST:
                first = g["own_f%d" % s] if d == 0 else g["cand_f%d" % s].at[d]
                local[d, s] = first[0, pl.ds(r0, rows), :]
            for j, s in enumerate(slots):
                local[d, s] = g["own_" + name][j] if d == 0 else g["cand_" + name][d, j]
        wire, size = g["wireout_" + name], g["sizeout_" + name]
        for dz in range(1, ZN):
            sums = sums_for(dz, local)
            for kk in range(2):
                top = jnp.maximum(jnp.max(jnp.abs(sums[kk]), axis=0, keepdims=True), 1e-30)
                size[dz, pl.ds(kk, 1), :] = top * (1.0 / LEVELS)
                wire[dz, kk] = jnp.round(sums[kk] * (LEVELS / top)).astype(jnp.int32).astype(jnp.int16)
            go(wire.at[dz], g["wire_" + name].at[dz], "wire_" + name, dz, zdev(dz))
            go(size.at[dz], g["size_" + name].at[dz], "size_" + name, dz, zdev(dz))
        sums = sums_for(0, local)
        for kk in range(2):
            out[kk, 0, pl.ds(r0, rows), :] = sums[kk]

    def finish(c):
        name, slots, r0, rows = units[len(FIRST) + c]
        wire, size = g["wire_" + name], g["size_" + name]
        sums = [out[kk, 0, pl.ds(r0, rows), :] for kk in range(2)]
        for dz in range(1, ZN):
            copy_to(g["wireout_" + name].at[dz], wire.at[dz], "wire_" + name, dz, zdev(dz)).wait_recv()
            copy_to(g["sizeout_" + name].at[dz], size.at[dz], "size_" + name, dz, zdev(dz)).wait_recv()
            for kk in range(2):
                scale = size[dz, pl.ds(kk, 1), :]
                sums[kk] = sums[kk] + wire[dz, kk].astype(jnp.int32).astype(F32) * scale
        for kk in range(2):
            out[kk, 0, pl.ds(r0, rows), :] = sums[kk]

    for s in range(CAP):
        spread(s, 0)
        if s == 0:
            near_out(0)
    near_in(0, 0)
    loads[0].wait()
    compute("f0", 0, 0, 0, 128, PAIRS[:1])
    near_on(0)
    near_out(1)
    compute("f0", 0, 0, 0, 128, PAIRS[1:2])
    near_out(2)
    for s in range(CAP):
        spread(s, 1)
    near_in(0, 2)
    compute("f0", 0, 0, 0, 128, PAIRS[2:3])
    near_on(1)
    near_out(3)
    near_in(0, 1, 3)
    compute("f0", 0, 0, 0, 128, PAIRS[3:])
    sib_out("f0")
    near_on(2)
    near_in(1, 0, 1, 2, 3)
    loads[1].wait()
    c0, c1, c2, c3 = units[len(FIRST):]

    def slot(unit, j):
        name, slots, r0, rows = unit
        compute(name, slots[j], j, r0, rows)

    slot(c0, 0)
    near_on(3)
    x_out("f0")
    near_in(2, 0, 1, 2, 3)
    loads[2].wait()
    slot(c0, 1)
    near_in(3, 0, 1, 2, 3)
    loads[3].wait()
    for s in range(CAP):
        g["far%d" % s][...] = collect(s, 1)
    make_routes()
    slot(c0, 2)
    sib_out(c0[0])
    y_out(*units[0])
    slot(c1, 0)
    x_out(c0[0])
    slot(c1, 1)
    slot(c1, 2)
    sib_out(c1[0])
    y_out(*c0)
    y_in("f0")
    slot(c2, 0)
    x_out(c1[0])
    slot(c2, 1)
    z_out(0)
    slot(c2, 2)
    sib_out(c2[0])
    y_out(*c1)
    slot(c3, 0)
    slot(c3, 1)
    x_out(c2[0])
    slot(c3, 2)
    sib_out(c3[0])
    z_out(1)
    y_out(*c2)
    x_out(c3[0])
    finish(0)
    y_out(*c3)
    z_out(2)
    z_out(3)
    finish(1)
    finish(2)
    finish(3)
    for copy in sends:
        copy.wait_send()


SCRATCH = {}


def layout(aux, orb, listed, kpoints):
    dma = pltpu.SemaphoreType.DMA
    spec = {}

    def array(name, dims, dtype):
        spec[name] = pltpu.VMEM(dims, dtype)

    def pair(name, count):
        spec[name + "_s"] = dma((count,))
        spec[name + "_r"] = dma((count,))

    bf = jnp.bfloat16
    spec["trip"] = pltpu.SMEM((4, listed), jnp.int32)
    spec["diff"] = pltpu.SMEM((kpoints, kpoints), jnp.int32)
    spec["first_sem"] = dma((3,))
    spec["chol_sem"] = dma((CAP,))
    for d in range(ZN):
        array("ring%d" % d, (2, orb, orb), bf)
    array("pool", (2 * ZN, orb, orb), bf)
    pair("ring", 4 * ZN)
    for s in range(CAP):
        array("chol%d" % s, (aux, orb, orb), bf)
        for tag in "nf":
            array("%ssend%d" % (tag, s), (YN - 1, orb, orb), bf)
            array("%srecv%d" % (tag, s), (YN, orb, orb), bf)
        array("near%d" % s, (2, XN, orb, orb), bf)
        array("far%d" % s, (orb, orb), bf)
    for tag in "nf":
        pair(tag, CAP * YN)
    pair("x", CAP * XN)
    pair("w", CAP * XN)
    units = [("f%d" % s, 1, orb) for s in FIRST]
    units += [("c%d" % c, len(LAST), rows) for c, (_, rows) in enumerate(CHUNKS)]
    for name, slots, rows in units:
        for kind in ("keep_", "give_", "sib_", "sums_", "xr_"):
            array(kind + name, (XN, slots, rows, orb), F32)
        array("own_" + name, (slots, rows, orb), F32)
        array("cand_" + name, (YN, slots, rows, orb), F32)
        pair("sib_" + name, 1)
        pair("xr_" + name, XN)
        pair("cand_" + name, YN)
        if name[0] == "c":
            array("local_" + name, (YN, CAP, rows, orb), F32)
            for kind in ("wireout_", "wire_"):
                array(kind + name, (ZN, 2, rows, orb), jnp.int16)
            for kind in ("sizeout_", "size_"):
                array(kind + name, (ZN, 8, orb), F32)
            pair("wire_" + name, ZN)
            pair("size_" + name, ZN)
    spec["tab"] = pltpu.SMEM((YN * CAP * 4,), jnp.int32)
    spec["route"] = pltpu.SMEM((ZN * YN,), jnp.int32)
    return spec


def on_device(green, chol, triplets, diff):
    aux, orb = chol.shape[1], chol.shape[3]
    spec = layout(aux, orb, triplets.shape[0], diff.shape[0])
    SCRATCH.clear()
    SCRATCH.update(spec)
    return pl.pallas_call(
        kernel,
        out_shape=jax.ShapeDtypeStruct((2, 1, orb, orb), F32),
        in_specs=[pl.BlockSpec(memory_space=pltpu.HBM)] * 4,
        out_specs=pl.BlockSpec(memory_space=pltpu.VMEM),
        scratch_shapes=list(spec.values()),
        compiler_params=pltpu.CompilerParams(
            collective_id=0, has_side_effects=True, vmem_limit_bytes=64 * 2**20 - 2**17
        ),
    )(triplets.T, diff, green, chol)


def solution(mesh):
    in_specs = (P("ka", "tau", None, None), P("ka", "tau", None, None), P(), P())
    out_specs = P("ka", "tau", None, None)
    return jax.shard_map(
        on_device, mesh=mesh, in_specs=in_specs, out_specs=out_specs, check_vma=False
    )
```

```python
import jax
import jax.numpy as jnp
from jax import lax
from jax.experimental import pallas as pl
from jax.experimental.pallas import tpu as pltpu
from jax.sharding import PartitionSpec as P

MESH = pl.DeviceIdType.MESH
ZN, YN, XN, CAP = 8, 4, 4, 4
F32 = jnp.float32
FIRST = (0,)
LAST = (1, 2, 3)
CHUNKS = ((0, 32), (32, 32), (64, 32), (96, 16), (112, 16))
LEVELS = 32766.0
ZORDER = (4, 3, 5, 2, 6, 1, 7)
PAIRS = (((0, 0), (1, 0)), ((0, 1), (0, 3)), ((0, 2), (1, 2)), ((1, 1), (1, 3)))


def pack(blocks, wire, size, at):
    for i, block in enumerate(blocks):
        top = jnp.maximum(jnp.max(jnp.abs(block), axis=0, keepdims=True), 1e-30)
        size[at, pl.ds(i, 1), :] = top * (1.0 / LEVELS)
        wire[at, i] = jnp.round(block * (LEVELS / top)).astype(jnp.int32).astype(jnp.int16)


def unpack(wire, size, at, i):
    return wire[at, i].astype(jnp.int32).astype(F32) * size[at, pl.ds(i, 1), :]


def contract_pair(vectors, near, results, pair, at, step, row):
    x = vectors[:, pl.ds(at, step), :]
    count, _, width = x.shape
    weight = jnp.concatenate([near[e, d] for e, d in pair], axis=1)
    product = jnp.dot(
        x.reshape(count * step, width), weight, preferred_element_type=F32
    ).reshape(count, step, 2 * width)
    wide = x.astype(F32)
    total = jnp.zeros((step, 2 * width), F32)
    for q in range(count):
        total = total + product[q] * jnp.concatenate([wide[q], wide[q]], axis=1)
    for i, (e, d) in enumerate(pair):
        results[e][d, pl.ds(row, step), :] = total[:, i * width : (i + 1) * width]


def kernel(trip_hbm, diff_hbm, green, chol, out, *scratch):
    g = dict(zip(list(SCRATCH), scratch))
    ka = lax.axis_index("ka")
    tau = lax.axis_index("tau")
    z, y = ka // YN, ka % YN
    x, core = tau // 2, tau % 2
    units = [("f%d" % s, (s,), 0, 128) for s in FIRST]
    units += [("c%d" % c, LAST, r0, rows) for c, (r0, rows) in enumerate(CHUNKS)]

    def zdev(d):
        return {"ka": (z + d) % ZN * YN + y}

    def ydev(d):
        return {"ka": z * YN + (y + d) % YN}

    def xdev(d):
        return {"tau": (x + d) % XN * 2 + core}

    sibling = {"tau": x * 2 + 1 - core}

    barrier = pltpu.get_barrier_semaphore()
    peers = [zdev(d) for d in range(1, ZN)] + [ydev(d) for d in range(1, YN)]
    peers += [xdev(d) for d in range(1, XN)] + [sibling]
    ring = [g["ring%d" % d] for d in range(ZN)]
    trip, diff = g["trip"], g["diff"]
    first_loads = [
        pltpu.make_async_copy(green.at[:, 0], ring[0], g["first_sem"].at[0]),
        pltpu.make_async_copy(trip_hbm, trip, g["first_sem"].at[1]),
        pltpu.make_async_copy(diff_hbm, diff, g["first_sem"].at[2]),
    ]
    loads = [
        pltpu.make_async_copy(chol.at[s], g["chol%d" % s], g["chol_sem"].at[s]) for s in range(CAP)
    ]
    for peer in peers:
        pl.semaphore_signal(barrier, inc=1, device_id=peer, device_id_type=MESH)
    for load in first_loads + loads:
        load.start()
    for load in first_loads:
        load.wait()
    pl.semaphore_wait(barrier, len(peers))

    sends = []

    def copy_to(src, dst, name, index, where):
        return pltpu.make_async_remote_copy(
            src_ref=src, dst_ref=dst, send_sem=g[name + "_s"].at[index], recv_sem=g[name + "_r"].at[index],
            device_id=where, device_id_type=MESH,
        )

    def go(*args):
        copy = copy_to(*args)
        copy.start()
        sends.append(copy)

    def hop(way, step, kk):
        if way == 0:
            src, dst, to = ring[step - 1], ring[step], zdev(1)
        else:
            src, dst, to = ring[(ZN + 1 - step) % ZN], ring[ZN - step], zdev(ZN - 1)
        return src.at[kk], dst.at[kk], "ring", (way * ZN + step) * 2 + kk, to

    def hops(step):
        if step < ZN // 2:
            return [(way, step, kk) for kk in range(2) for way in range(2)]
        return [(0, step, 0), (1, step, 1)]

    for args in hops(1):
        go(*hop(*args))

    def scan(t, carry):
        counts, found = carry
        owner = trip[3, t]
        row_hit = (owner // YN) == z
        rel = (owner % YN + YN - y) % YN
        new_counts, new_found = [], []
        for j in range(YN):
            hit = row_hit & (rel == j)
            for s in range(CAP):
                new_found.append(jnp.where(hit & (counts[j] == s), t, found[j * CAP + s]))
            new_counts.append(counts[j] + hit.astype(jnp.int32))
        return tuple(new_counts), tuple(new_found)

    zero = jnp.int32(0)
    state = ((zero,) * YN, (zero,) * (YN * CAP))
    rows_of = trip.shape[1]
    half = ZN // 2
    for step in range(1, half + 1):
        state = lax.fori_loop((step - 1) * rows_of // half, step * rows_of // half, scan, state)
        if step < half:
            ahead = hops(step + 1)
            for way, _, kk in hops(step):
                copy_to(*hop(way, step, kk)).wait_recv()
                if (way, step + 1, kk) in ahead:
                    go(*hop(way, step + 1, kk))
    counts, found = state
    tab = g["tab"]
    firsts = []
    for j in range(YN):
        for s in range(CAP):
            row = found[j * CAP + s]
            k1, k2, k3 = trip[0, row], trip[1, row], trip[2, row]
            for which, k in enumerate((k2, diff[k1, diff[k2, k3]])):
                tab[((j * CAP + s) * 2 + which) * 2] = (z + ZN - k // (2 * YN)) % ZN * 2 + k % 2
                tab[((j * CAP + s) * 2 + which) * 2 + 1] = (y + YN - k // 2 % YN) % YN
            firsts.append(jnp.where(counts[j] > s, k1, -1))
    for way, step, kk in hops(half):
        copy_to(*hop(way, step, kk)).wait_recv()
    pool = g["pool"]
    for d in range(ZN):
        for kk in range(2):
            pool[2 * d + kk] = ring[d][kk]

    def pick(j, s, which):
        return pool[tab[((j * CAP + s) * 2 + which) * 2]]

    def spread(s, which):
        tag = "nf"[which]
        send, recv = g["%ssend%d" % (tag, s)], g["%srecv%d" % (tag, s)]
        for d in range(1, YN):
            send[d - 1] = pick(d, s, which)
            go(send.at[d - 1], recv.at[d], tag, s * YN + d, ydev(d))
        recv[0] = pick(0, s, which)

    def collect(s, which):
        tag = "nf"[which]
        send, recv = g["%ssend%d" % (tag, s)], g["%srecv%d" % (tag, s)]
        for d in range(1, YN):
            copy_to(send.at[d - 1], recv.at[d], tag, s * YN + d, ydev(d)).wait_recv()
        rel = tab[(s * 2 + which) * 2 + 1]
        block = recv[0]
        for d in range(1, YN):
            block = jnp.where(rel == d, recv[d], block)
        return block

    near = [g["near%d" % s] for s in range(CAP)]

    def near_out(s):
        near[s][0, 0] = collect(s, 0)
        go(near[s].at[0, 0], near[s].at[1, 0], "w", s * XN, sibling)
        for d in (1, XN - 1, 2):
            go(near[s].at[0, 0], near[s].at[0, d], "x", s * XN + d, xdev(d))

    def near_on(s):
        for d in (1, XN - 1, 2):
            copy_to(near[s].at[0, 0], near[s].at[0, d], "x", s * XN + d, xdev(d)).wait_recv()
            go(near[s].at[0, d], near[s].at[1, d], "w", s * XN + d, sibling)

    def near_in(s, *ds):
        for d in ds:
            copy_to(near[s].at[0, d], near[s].at[1, d], "w", s * XN + d, sibling).wait_recv()

    def compute(name, s, j, r0, rows, pairs=PAIRS):
        results = [g[k + name].at[:, j] for k in ("keep_", "give_")]
        for pair in pairs:
            for row in range(0, rows, 16):
                contract_pair(g["chol%d" % s], near[s], results, pair, r0 + row, 16, row)

    def sib_out(name):
        go(g["give_" + name], g["sib_" + name], "sib_" + name, 0, sibling)

    def mail(kind, name, src, dst, where):
        go(g[kind + "wo_" + name].at[src], g[kind + "wi_" + name].at[dst], kind + "w_" + name, dst, where)
        go(g[kind + "so_" + name].at[src], g[kind + "si_" + name].at[dst], kind + "s_" + name, dst, where)

    def get(kind, name, src, dst, where):
        copy_to(
            g[kind + "wo_" + name].at[src], g[kind + "wi_" + name].at[dst], kind + "w_" + name, dst, where
        ).wait_recv()
        copy_to(
            g[kind + "so_" + name].at[src], g[kind + "si_" + name].at[dst], kind + "s_" + name, dst, where
        ).wait_recv()

    def put(kind, name, src, blocks):
        pack(blocks, g[kind + "wo_" + name], g[kind + "so_" + name], src)

    def read(kind, name, dst, i):
        return unpack(g[kind + "wi_" + name], g[kind + "si_" + name], dst, i)

    def x_out(name):
        keep, sib = g["keep_" + name], g["sib_" + name]
        copy_to(g["give_" + name], sib, "sib_" + name, 0, sibling).wait_recv()
        for d in (2, 1, XN - 1):
            put("x", name, d, [keep[d, j] + sib[d, j] for j in range(keep.shape[1])])
            mail("x", name, d, d, xdev(XN - d))

    def y_out(name, slots, r0, rows):
        keep, own = g["keep_" + name], g["own_" + name]
        totals = [keep[0, j] + g["sib_" + name][0, j] for j in range(len(slots))]
        for d in range(1, XN):
            get("x", name, d, d, xdev(XN - d))
            totals = [total + read("x", name, d, j) for j, total in enumerate(totals)]
        for j, s in enumerate(slots):
            own[j] = totals[j] * g["far%d" % s][pl.ds(r0, rows), :].astype(F32)
        put("y", name, 0, [own[j] for j in range(len(slots))])
        for d in (2, 1, YN - 1):
            mail("y", name, 0, d, ydev(d))

    def y_in(name):
        for d in range(1, YN):
            get("y", name, 0, d, ydev(d))

    route = g["route"]

    def make_routes():
        for dz in range(ZN):
            target = (z + dz) % ZN * YN + y
            for d in range(YN):
                j = (YN - d) % YN
                code = jnp.int32(8)
                for s in range(CAP):
                    k1 = firsts[j * CAP + s]
                    code = jnp.where((k1 >= 0) & ((k1 // 2) == target), s * 2 + k1 % 2, code)
                route[dz * YN + d] = code

    def sums_for(dz, local):
        sums = [jnp.zeros(local.shape[2:], F32) for _ in range(2)]
        for d in range(YN):
            code = route[dz * YN + d]
            block = local[d, (code % 8) // 2]
            for kk in range(2):
                sums[kk] = sums[kk] + jnp.where((code < 8) & (code % 2 == kk), block, 0.0)
        return sums

    def z_out(c):
        name, slots, r0, rows = units[len(FIRST) + c]
        y_in(name)
        local = g["local_" + name]
        for d in range(YN):
            for s in FIRST:
                if d == 0:
                    local[d, s] = g["own_f%d" % s][0, pl.ds(r0, rows), :]
                else:
                    scale = g["ysi_f%d" % s][d, pl.ds(0, 1), :]
                    part = g["ywi_f%d" % s][d, 0, pl.ds(r0, rows), :]
                    local[d, s] = part.astype(jnp.int32).astype(F32) * scale
            for j, s in enumerate(slots):
                local[d, s] = g["own_" + name][j] if d == 0 else read("y", name, d, j)
        for dz in ZORDER:
            put("z", name, dz, sums_for(dz, local))
            mail("z", name, dz, dz, zdev(dz))
        sums = sums_for(0, local)
        for kk in range(2):
            out[kk, 0, pl.ds(r0, rows), :] = sums[kk]

    def finish(c):
        name, slots, r0, rows = units[len(FIRST) + c]
        sums = [out[kk, 0, pl.ds(r0, rows), :] for kk in range(2)]
        for dz in range(1, ZN):
            get("z", name, dz, dz, zdev(dz))
            for kk in range(2):
                sums[kk] = sums[kk] + read("z", name, dz, kk)
        for kk in range(2):
            out[kk, 0, pl.ds(r0, rows), :] = sums[kk]

    for s in range(CAP):
        spread(s, 0)
        if s == 0:
            near_out(0)
    near_in(0, 0)
    loads[0].wait()
    compute("f0", 0, 0, 0, 128, PAIRS[:1])
    near_on(0)
    near_out(1)
    compute("f0", 0, 0, 0, 128, PAIRS[1:2])
    near_out(2)
    for s in range(CAP):
        spread(s, 1)
    near_in(0, 2)
    compute("f0", 0, 0, 0, 128, PAIRS[2:3])
    near_on(1)
    near_out(3)
    near_in(0, 1, 3)
    compute("f0", 0, 0, 0, 128, PAIRS[3:])
    sib_out("f0")
    near_on(2)
    near_in(1, 0, 1, 2, 3)
    loads[1].wait()
    c0, c1, c2, c3, c4 = units[len(FIRST):]

    def slot(unit, j):
        name, slots, r0, rows = unit
        compute(name, slots[j], j, r0, rows)

    def end_part(*pairs):
        name, slots, r0, rows = c4
        for j, s in enumerate(slots):
            compute(name, s, j, r0, rows, pairs)

    slot(c0, 0)
    near_on(3)
    x_out("f0")
    near_in(2, 0, 1, 2, 3)
    loads[2].wait()
    slot(c0, 1)
    near_in(3, 0, 1, 2, 3)
    loads[3].wait()
    for s in range(CAP):
        g["far%d" % s][...] = collect(s, 1)
    make_routes()
    slot(c0, 2)
    sib_out(c0[0])
    y_out(*units[0])
    slot(c1, 0)
    x_out(c0[0])
    slot(c1, 1)
    y_in("f0")
    slot(c1, 2)
    sib_out(c1[0])
    slot(c2, 0)
    y_out(*c0)
    x_out(c1[0])
    slot(c2, 1)
    slot(c2, 2)
    sib_out(c2[0])
    z_out(0)
    slot(c3, 0)
    y_out(*c1)
    slot(c3, 1)
    x_out(c2[0])
    slot(c3, 2)
    sib_out(c3[0])
    end_part(PAIRS[3], PAIRS[2])
    x_out(c3[0])
    z_out(1)
    end_part(PAIRS[0])
    sib_out(c4[0])
    y_out(*c2)
    end_part(PAIRS[1])
    x_out(c4[0])
    y_out(*c3)
    z_out(2)
    finish(0)
    y_out(*c4)
    z_out(3)
    z_out(4)
    for c in range(1, len(CHUNKS)):
        finish(c)
    for copy in sends:
        copy.wait_send()


SCRATCH = {}


def layout(aux, orb, listed, kpoints):
    dma = pltpu.SemaphoreType.DMA
    spec = {}

    def array(name, dims, dtype):
        spec[name] = pltpu.VMEM(dims, dtype)

    def pair(name, count):
        spec[name + "_s"] = dma((count,))
        spec[name + "_r"] = dma((count,))

    bf = jnp.bfloat16
    spec["trip"] = pltpu.SMEM((4, listed), jnp.int32)
    spec["diff"] = pltpu.SMEM((kpoints, kpoints), jnp.int32)
    spec["first_sem"] = dma((3,))
    spec["chol_sem"] = dma((CAP,))
    for d in range(ZN):
        array("ring%d" % d, (2, orb, orb), bf)
    array("pool", (2 * ZN, orb, orb), bf)
    pair("ring", 4 * ZN)
    for s in range(CAP):
        array("chol%d" % s, (aux, orb, orb), bf)
        for tag in "nf":
            array("%ssend%d" % (tag, s), (YN - 1, orb, orb), bf)
            array("%srecv%d" % (tag, s), (YN, orb, orb), bf)
        array("near%d" % s, (2, XN, orb, orb), bf)
        array("far%d" % s, (orb, orb), bf)
    for tag in "nf":
        pair(tag, CAP * YN)
    pair("x", CAP * XN)
    pair("w", CAP * XN)
    units = [("f%d" % s, 1, orb) for s in FIRST]
    units += [("c%d" % c, len(LAST), rows) for c, (_, rows) in enumerate(CHUNKS)]
    for name, slots, rows in units:
        for kind in ("keep_", "give_", "sib_"):
            array(kind + name, (XN, slots, rows, orb), F32)
        array("own_" + name, (slots, rows, orb), F32)
        pair("sib_" + name, 1)
        mails = [("x", XN, slots), ("y", YN, slots)]
        if name[0] == "c":
            array("local_" + name, (YN, CAP, rows, orb), F32)
            mails.append(("z", ZN, 2))
        for kind, count, blocks in mails:
            for way in "oi":
                array(kind + "w" + way + "_" + name, (count, blocks, rows, orb), jnp.int16)
                array(kind + "s" + way + "_" + name, (count, 4 if blocks > 2 else blocks, orb), F32)
            pair(kind + "w_" + name, count)
            pair(kind + "s_" + name, count)
    spec["tab"] = pltpu.SMEM((YN * CAP * 4,), jnp.int32)
    spec["route"] = pltpu.SMEM((ZN * YN,), jnp.int32)
    return spec


def on_device(green, chol, triplets, diff):
    aux, orb = chol.shape[1], chol.shape[3]
    spec = layout(aux, orb, triplets.shape[0], diff.shape[0])
    SCRATCH.clear()
    SCRATCH.update(spec)
    return pl.pallas_call(
        kernel,
        out_shape=jax.ShapeDtypeStruct((2, 1, orb, orb), F32),
        in_specs=[pl.BlockSpec(memory_space=pltpu.HBM)] * 4,
        out_specs=pl.BlockSpec(memory_space=pltpu.VMEM),
        scratch_shapes=list(spec.values()),
        compiler_params=pltpu.CompilerParams(
            collective_id=0, has_side_effects=True, vmem_limit_bytes=64 * 2**20 - 2**17
        ),
    )(triplets.T, diff, green, chol)


def solution(mesh):
    in_specs = (P("ka", "tau", None, None), P("ka", "tau", None, None), P(), P())
    out_specs = P("ka", "tau", None, None)
    return jax.shard_map(
        on_device, mesh=mesh, in_specs=in_specs, out_specs=out_specs, check_vma=False
    )
```

```python
import jax
import jax.numpy as jnp
from jax import lax
from jax.experimental import pallas as pl
from jax.experimental.pallas import tpu as pltpu
from jax.sharding import PartitionSpec as P

MESH = pl.DeviceIdType.MESH
ZN, YN, XN, CAP = 8, 4, 4, 4
F32 = jnp.float32
FIRST = (0,)
LAST = (1, 2, 3)
CHUNKS = ((0, 32), (32, 32), (64, 32), (96, 16), (112, 16))
LEVELS = 32766.0
ZORDER = (4, 3, 5, 2, 6, 1, 7)
PAIRS = (((0, 0), (1, 0)), ((0, 1), (0, 3)), ((0, 2), (1, 2)), ((1, 1), (1, 3)))


def pack(blocks, wire, size, at):
    for i, block in enumerate(blocks):
        top = jnp.maximum(jnp.max(jnp.abs(block), axis=0, keepdims=True), 1e-30)
        size[at, pl.ds(i, 1), :] = top * (1.0 / LEVELS)
        wire[at, i] = jnp.round(block * (LEVELS / top)).astype(jnp.int32).astype(jnp.int16)


def unpack(wire, size, at, i):
    return wire[at, i].astype(jnp.int32).astype(F32) * size[at, pl.ds(i, 1), :]


def contract_pair(vectors, near, results, pair, at, step, row):
    x = vectors[:, pl.ds(at, step), :]
    count, _, width = x.shape
    weight = jnp.concatenate([near[e, d] for e, d in pair], axis=1)
    product = jnp.dot(
        x.reshape(count * step, width), weight, preferred_element_type=F32
    ).reshape(count, step, 2 * width)
    wide = x.astype(F32)
    total = jnp.zeros((step, 2 * width), F32)
    for q in range(count):
        total = total + product[q] * jnp.concatenate([wide[q], wide[q]], axis=1)
    for i, (e, d) in enumerate(pair):
        results[e][d, pl.ds(row, step), :] = total[:, i * width : (i + 1) * width]


def kernel(trip_hbm, diff_hbm, green, chol, out, *scratch):
    g = dict(zip(list(SCRATCH), scratch))
    ka = lax.axis_index("ka")
    tau = lax.axis_index("tau")
    z, y = ka // YN, ka % YN
    x, core = tau // 2, tau % 2
    units = [("f%d" % s, (s,), 0, 128) for s in FIRST]
    units += [("c%d" % c, LAST, r0, rows) for c, (r0, rows) in enumerate(CHUNKS)]

    def zdev(d):
        return {"ka": (z + d) % ZN * YN + y}

    def ydev(d):
        return {"ka": z * YN + (y + d) % YN}

    def xdev(d):
        return {"tau": (x + d) % XN * 2 + core}

    sibling = {"tau": x * 2 + 1 - core}

    barrier = pltpu.get_barrier_semaphore()
    peers = [zdev(d) for d in range(1, ZN)] + [ydev(d) for d in range(1, YN)]
    peers += [xdev(d) for d in range(1, XN)] + [sibling]
    ring = [g["ring%d" % d] for d in range(ZN)]
    trip, diff = g["trip"], g["diff"]
    first_loads = [
        pltpu.make_async_copy(green.at[:, 0], ring[0], g["first_sem"].at[0]),
        pltpu.make_async_copy(trip_hbm, trip, g["first_sem"].at[1]),
        pltpu.make_async_copy(diff_hbm, diff, g["first_sem"].at[2]),
    ]
    loads = [
        pltpu.make_async_copy(chol.at[s], g["chol%d" % s], g["chol_sem"].at[s]) for s in range(CAP)
    ]
    for load in first_loads:
        load.start()
    for peer in peers:
        pl.semaphore_signal(barrier, inc=1, device_id=peer, device_id_type=MESH)
    for load in loads:
        load.start()
    for load in first_loads:
        load.wait()
    pl.semaphore_wait(barrier, len(peers))

    sends = []

    def copy_to(src, dst, name, index, where):
        return pltpu.make_async_remote_copy(
            src_ref=src, dst_ref=dst, send_sem=g[name + "_s"].at[index], recv_sem=g[name + "_r"].at[index],
            device_id=where, device_id_type=MESH,
        )

    def go(*args):
        copy = copy_to(*args)
        copy.start()
        sends.append(copy)

    def hop(src, dst, kk):
        return ring[src].at[kk], ring[dst].at[kk], "ring", dst * 2 + kk, zdev((dst + ZN - src) % ZN)

    near_by = [(0, d, kk) for kk in range(2) for d in (2, ZN - 2)]
    near_by += [(0, d, kk) for kk in range(2) for d in (1, ZN - 1)]
    onward = [(2, 3, 0), (2, 4, 0), (ZN - 2, ZN - 3, 0), (2, 3, 1), (ZN - 2, ZN - 3, 1), (ZN - 2, 4, 1)]
    for args in near_by:
        go(*hop(*args))

    def scan(t, carry):
        counts, found = carry
        owner = trip[3, t]
        row_hit = (owner // YN) == z
        rel = (owner % YN + YN - y) % YN
        new_counts, new_found = [], []
        for j in range(YN):
            hit = row_hit & (rel == j)
            for s in range(CAP):
                new_found.append(jnp.where(hit & (counts[j] == s), t, found[j * CAP + s]))
            new_counts.append(counts[j] + hit.astype(jnp.int32))
        return tuple(new_counts), tuple(new_found)

    zero = jnp.int32(0)
    state = ((zero,) * YN, (zero,) * (YN * CAP))
    rows_of = trip.shape[1]
    state = lax.fori_loop(0, rows_of // 2, scan, state)
    for _, d, kk in near_by[:4]:
        copy_to(*hop(0, d, kk)).wait_recv()
        for args in onward:
            if args[0] == d and args[2] == kk:
                go(*hop(*args))
    state = lax.fori_loop(rows_of // 2, rows_of, scan, state)
    counts, found = state
    tab = g["tab"]
    firsts = []
    for j in range(YN):
        for s in range(CAP):
            row = found[j * CAP + s]
            k1, k2, k3 = trip[0, row], trip[1, row], trip[2, row]
            for which, k in enumerate((k2, diff[k1, diff[k2, k3]])):
                tab[((j * CAP + s) * 2 + which) * 2] = (z + ZN - k // (2 * YN)) % ZN * 2 + k % 2
                tab[((j * CAP + s) * 2 + which) * 2 + 1] = (y + YN - k // 2 % YN) % YN
            firsts.append(jnp.where(counts[j] > s, k1, -1))
    for args in near_by[4:] + onward:
        copy_to(*hop(*args)).wait_recv()
    pool = g["pool"]
    for d in range(ZN):
        for kk in range(2):
            pool[2 * d + kk] = ring[d][kk]

    def pick(j, s, which):
        return pool[tab[((j * CAP + s) * 2 + which) * 2]]

    def spread(s, which):
        tag = "nf"[which]
        send, recv = g["%ssend%d" % (tag, s)], g["%srecv%d" % (tag, s)]
        for d in range(1, YN):
            send[d - 1] = pick(d, s, which)
            go(send.at[d - 1], recv.at[d], tag, s * YN + d, ydev(d))
        recv[0] = pick(0, s, which)

    def collect(s, which):
        tag = "nf"[which]
        send, recv = g["%ssend%d" % (tag, s)], g["%srecv%d" % (tag, s)]
        for d in range(1, YN):
            copy_to(send.at[d - 1], recv.at[d], tag, s * YN + d, ydev(d)).wait_recv()
        rel = tab[(s * 2 + which) * 2 + 1]
        block = recv[0]
        for d in range(1, YN):
            block = jnp.where(rel == d, recv[d], block)
        return block

    near = [g["near%d" % s] for s in range(CAP)]

    def near_out(s):
        near[s][0, 0] = collect(s, 0)
        go(near[s].at[0, 0], near[s].at[1, 0], "w", s * XN, sibling)
        for d in (1, XN - 1, 2):
            go(near[s].at[0, 0], near[s].at[0, d], "x", s * XN + d, xdev(d))

    def near_on(s):
        for d in (1, XN - 1, 2):
            copy_to(near[s].at[0, 0], near[s].at[0, d], "x", s * XN + d, xdev(d)).wait_recv()
            go(near[s].at[0, d], near[s].at[1, d], "w", s * XN + d, sibling)

    def near_in(s, *ds):
        for d in ds:
            copy_to(near[s].at[0, d], near[s].at[1, d], "w", s * XN + d, sibling).wait_recv()

    def compute(name, s, j, r0, rows, pairs=PAIRS):
        results = [g[k + name].at[:, j] for k in ("keep_", "give_")]
        for pair in pairs:
            for row in range(0, rows, 16):
                contract_pair(g["chol%d" % s], near[s], results, pair, r0 + row, 16, row)

    def sib_out(name):
        go(g["give_" + name], g["sib_" + name], "sib_" + name, 0, sibling)

    def mail(kind, name, src, dst, where):
        go(g[kind + "wo_" + name].at[src], g[kind + "wi_" + name].at[dst], kind + "w_" + name, dst, where)
        go(g[kind + "so_" + name].at[src], g[kind + "si_" + name].at[dst], kind + "s_" + name, dst, where)

    def get(kind, name, src, dst, where):
        copy_to(
            g[kind + "wo_" + name].at[src], g[kind + "wi_" + name].at[dst], kind + "w_" + name, dst, where
        ).wait_recv()
        copy_to(
            g[kind + "so_" + name].at[src], g[kind + "si_" + name].at[dst], kind + "s_" + name, dst, where
        ).wait_recv()

    def put(kind, name, src, blocks):
        pack(blocks, g[kind + "wo_" + name], g[kind + "so_" + name], src)

    def read(kind, name, dst, i):
        return unpack(g[kind + "wi_" + name], g[kind + "si_" + name], dst, i)

    def x_out(name):
        keep, sib = g["keep_" + name], g["sib_" + name]
        copy_to(g["give_" + name], sib, "sib_" + name, 0, sibling).wait_recv()
        for d in (2, 1, XN - 1):
            put("x", name, d, [keep[d, j] + sib[d, j] for j in range(keep.shape[1])])
            mail("x", name, d, d, xdev(XN - d))

    def y_out(name, slots, r0, rows):
        keep, own = g["keep_" + name], g["own_" + name]
        totals = [keep[0, j] + g["sib_" + name][0, j] for j in range(len(slots))]
        for d in range(1, XN):
            get("x", name, d, d, xdev(XN - d))
            totals = [total + read("x", name, d, j) for j, total in enumerate(totals)]
        for j, s in enumerate(slots):
            own[j] = totals[j] * g["far%d" % s][pl.ds(r0, rows), :].astype(F32)
        put("y", name, 0, [own[j] for j in range(len(slots))])
        for d in (2, 1, YN - 1):
            mail("y", name, 0, d, ydev(d))

    def y_in(name):
        for d in range(1, YN):
            get("y", name, 0, d, ydev(d))

    route = g["route"]

    def make_routes():
        for dz in range(ZN):
            target = (z + dz) % ZN * YN + y
            for d in range(YN):
                j = (YN - d) % YN
                code = jnp.int32(8)
                for s in range(CAP):
                    k1 = firsts[j * CAP + s]
                    code = jnp.where((k1 >= 0) & ((k1 // 2) == target), s * 2 + k1 % 2, code)
                route[dz * YN + d] = code

    def sums_for(dz, local):
        sums = [jnp.zeros(local.shape[2:], F32) for _ in range(2)]
        for d in range(YN):
            code = route[dz * YN + d]
            block = local[d, (code % 8) // 2]
            for kk in range(2):
                sums[kk] = sums[kk] + jnp.where((code < 8) & (code % 2 == kk), block, 0.0)
        return sums

    def z_out(c):
        name, slots, r0, rows = units[len(FIRST) + c]
        y_in(name)
        local = g["local_" + name]
        for d in range(YN):
            for s in FIRST:
                if d == 0:
                    local[d, s] = g["own_f%d" % s][0, pl.ds(r0, rows), :]
                else:
                    scale = g["ysi_f%d" % s][d, pl.ds(0, 1), :]
                    part = g["ywi_f%d" % s][d, 0, pl.ds(r0, rows), :]
                    local[d, s] = part.astype(jnp.int32).astype(F32) * scale
            for j, s in enumerate(slots):
                local[d, s] = g["own_" + name][j] if d == 0 else read("y", name, d, j)
        for dz in ZORDER:
            put("z", name, dz, sums_for(dz, local))
            mail("z", name, dz, dz, zdev(dz))
        sums = sums_for(0, local)
        for kk in range(2):
            out[kk, 0, pl.ds(r0, rows), :] = sums[kk]

    def finish(c):
        name, slots, r0, rows = units[len(FIRST) + c]
        sums = [out[kk, 0, pl.ds(r0, rows), :] for kk in range(2)]
        for dz in range(1, ZN):
            get("z", name, dz, dz, zdev(dz))
            for kk in range(2):
                sums[kk] = sums[kk] + read("z", name, dz, kk)
        for kk in range(2):
            out[kk, 0, pl.ds(r0, rows), :] = sums[kk]

    for s in range(CAP):
        spread(s, 0)
        if s == 0:
            near_out(0)
    near_in(0, 0)
    loads[0].wait()
    compute("f0", 0, 0, 0, 128, PAIRS[:1])
    near_on(0)
    near_out(1)
    compute("f0", 0, 0, 0, 128, PAIRS[1:2])
    near_out(2)
    for s in range(CAP):
        spread(s, 1)
    near_in(0, 2)
    compute("f0", 0, 0, 0, 128, PAIRS[2:3])
    near_on(1)
    near_out(3)
    near_in(0, 1, 3)
    compute("f0", 0, 0, 0, 128, PAIRS[3:])
    sib_out("f0")
    near_on(2)
    near_in(1, 0, 1, 2, 3)
    loads[1].wait()
    c0, c1, c2, c3, c4 = units[len(FIRST):]

    def slot(unit, j):
        name, slots, r0, rows = unit
        compute(name, slots[j], j, r0, rows)

    def end_part(*pairs):
        name, slots, r0, rows = c4
        for j, s in enumerate(slots):
            compute(name, s, j, r0, rows, pairs)

    slot(c0, 0)
    near_on(3)
    x_out("f0")
    near_in(2, 0, 1, 2, 3)
    loads[2].wait()
    slot(c0, 1)
    near_in(3, 0, 1, 2, 3)
    loads[3].wait()
    for s in range(CAP):
        g["far%d" % s][...] = collect(s, 1)
    make_routes()
    slot(c0, 2)
    sib_out(c0[0])
    y_out(*units[0])
    slot(c1, 0)
    x_out(c0[0])
    slot(c1, 1)
    y_in("f0")
    slot(c1, 2)
    sib_out(c1[0])
    slot(c2, 0)
    y_out(*c0)
    x_out(c1[0])
    slot(c2, 1)
    slot(c2, 2)
    sib_out(c2[0])
    z_out(0)
    slot(c3, 0)
    y_out(*c1)
    slot(c3, 1)
    x_out(c2[0])
    slot(c3, 2)
    sib_out(c3[0])
    end_part(PAIRS[3], PAIRS[2])
    x_out(c3[0])
    z_out(1)
    end_part(PAIRS[0])
    sib_out(c4[0])
    y_out(*c2)
    end_part(PAIRS[1])
    x_out(c4[0])
    y_out(*c3)
    z_out(2)
    finish(0)
    y_out(*c4)
    z_out(3)
    z_out(4)
    for c in range(1, len(CHUNKS)):
        finish(c)
    for copy in sends:
        copy.wait_send()


SCRATCH = {}


def layout(aux, orb, listed, kpoints):
    dma = pltpu.SemaphoreType.DMA
    spec = {}

    def array(name, dims, dtype):
        spec[name] = pltpu.VMEM(dims, dtype)

    def pair(name, count):
        spec[name + "_s"] = dma((count,))
        spec[name + "_r"] = dma((count,))

    bf = jnp.bfloat16
    spec["trip"] = pltpu.SMEM((4, listed), jnp.int32)
    spec["diff"] = pltpu.SMEM((kpoints, kpoints), jnp.int32)
    spec["first_sem"] = dma((3,))
    spec["chol_sem"] = dma((CAP,))
    for d in range(ZN):
        array("ring%d" % d, (2, orb, orb), bf)
    array("pool", (2 * ZN, orb, orb), bf)
    pair("ring", 4 * ZN)
    for s in range(CAP):
        array("chol%d" % s, (aux, orb, orb), bf)
        for tag in "nf":
            array("%ssend%d" % (tag, s), (YN - 1, orb, orb), bf)
            array("%srecv%d" % (tag, s), (YN, orb, orb), bf)
        array("near%d" % s, (2, XN, orb, orb), bf)
        array("far%d" % s, (orb, orb), bf)
    for tag in "nf":
        pair(tag, CAP * YN)
    pair("x", CAP * XN)
    pair("w", CAP * XN)
    units = [("f%d" % s, 1, orb) for s in FIRST]
    units += [("c%d" % c, len(LAST), rows) for c, (_, rows) in enumerate(CHUNKS)]
    for name, slots, rows in units:
        for kind in ("keep_", "give_", "sib_"):
            array(kind + name, (XN, slots, rows, orb), F32)
        array("own_" + name, (slots, rows, orb), F32)
        pair("sib_" + name, 1)
        mails = [("x", XN, slots), ("y", YN, slots)]
        if name[0] == "c":
            array("local_" + name, (YN, CAP, rows, orb), F32)
            mails.append(("z", ZN, 2))
        for kind, count, blocks in mails:
            for way in "oi":
                array(kind + "w" + way + "_" + name, (count, blocks, rows, orb), jnp.int16)
                array(kind + "s" + way + "_" + name, (count, 4 if blocks > 2 else blocks, orb), F32)
            pair(kind + "w_" + name, count)
            pair(kind + "s_" + name, count)
    spec["tab"] = pltpu.SMEM((YN * CAP * 4,), jnp.int32)
    spec["route"] = pltpu.SMEM((ZN * YN,), jnp.int32)
    return spec


def on_device(green, chol, triplets, diff):
    aux, orb = chol.shape[1], chol.shape[3]
    spec = layout(aux, orb, triplets.shape[0], diff.shape[0])
    SCRATCH.clear()
    SCRATCH.update(spec)
    return pl.pallas_call(
        kernel,
        out_shape=jax.ShapeDtypeStruct((2, 1, orb, orb), F32),
        in_specs=[pl.BlockSpec(memory_space=pltpu.HBM)] * 4,
        out_specs=pl.BlockSpec(memory_space=pltpu.VMEM),
        scratch_shapes=list(spec.values()),
        compiler_params=pltpu.CompilerParams(
            collective_id=0, has_side_effects=True, vmem_limit_bytes=64 * 2**20 - 2**17
        ),
    )(triplets.T, diff, green, chol)


def solution(mesh):
    in_specs = (P("ka", "tau", None, None), P("ka", "tau", None, None), P(), P())
    out_specs = P("ka", "tau", None, None)
    return jax.shard_map(
        on_device, mesh=mesh, in_specs=in_specs, out_specs=out_specs, check_vma=False
    )
```
